512 devices in a mesh: ctx: 32 (over z, core), head: 4 (over y), dp: 4 (over x).
Axes of the slice: x: 4, y: 4, z: 16, core: 2. Of those that a mesh axis runs over, the one named last changes fastest.
Arguments:
- latent: bfloat16 [4, 4096, 576], P('dp', 'ctx'), may hold values from -6 to 6
- queries: bfloat16 [4, 4096, 12288], P('dp', 'ctx', 'head'), may hold values from -330 to 330
- out_grad: bfloat16 [4, 4096, 8192], P('dp', 'ctx', 'head'), may hold values from -6 to 6
- segment_ids: int32 [4, 4096], P('dp', 'ctx'), may hold values from 0 to 31, never falling along the last dimension, each value on 1 to 256 neighbouring positions
- key_up: bfloat16 [512, 8192], P('dp', 'head'), may hold values from -0.25 to 0.25
- value_up: bfloat16 [512, 8192], P('dp', 'head'), may hold values from -0.25 to 0.25
Outputs:
- query_grad: bfloat16 [4, 4096, 12288], P('dp', 'ctx', 'head')
- latent_grad: bfloat16 [4, 4096, 576], P('dp', 'ctx')
- key_up_grad: float32 [512, 8192], P(('ctx', 'dp'), 'head')
The draws below stay inside these ranges and needn't reach their ends.
Inputs may be any that keep to these rules, and one draw needn't show every extreme that they name: `segment_ids`: segment numbers never fall along a trajectory; each segment holds at most 256 positions and one holds exactly 256.
All inputs are finite; a program needn't handle non-finite values.
Results may differ from the reference program's by a relative error of at most 0.0072.
Values may be sent and summed in bfloat16 or wider, within the bound.
A program may use at most 64 MiB of HBM per device.

```python
import math
import jax
import jax.numpy as jnp
import numpy as np
from jax import lax

D_LAT = 512
D_ROPE = 64
D_NOPE = 128
TOK_DEV = 128
HEADS = 64
SEQ = 4096
GROUPS = 4
REACH = 2
MOST = 256


def shared_rope(key):
    return jnp.clip(jax.random.normal(jax.random.fold_in(key, 11), (GROUPS, SEQ, D_ROPE), jnp.float32), -6.0, 6.0)


def draw_latent(key, part):
    rope_keys = shared_rope(key)
    key = jax.random.fold_in(key, 3)
    compressed = jnp.clip(jax.random.normal(key, (GROUPS, SEQ, D_LAT), jnp.float32), -6.0, 6.0)
    return jnp.concatenate([compressed, rope_keys], axis=-1).astype(jnp.bfloat16)


def draw_queries(key, part):
    key = jax.random.fold_in(key, 5)
    full_shape = (GROUPS, SEQ, HEADS, D_NOPE + D_ROPE)
    drawn = jnp.clip(jax.random.normal(key, full_shape, jnp.float32), -6.0, 6.0)
    return drawn.reshape(GROUPS, SEQ, HEADS * (D_NOPE + D_ROPE)).astype(jnp.bfloat16)


def steps_of(own_key, dims, cuts, least, high):
    def one(position, shards_of):
        steps = jax.random.uniform(jax.random.fold_in(jax.random.fold_in(own_key, 6), position), (shards_of,), jnp.float32, least / len(cuts), high / len(cuts))
        return jnp.repeat(jnp.exp(steps), dims[position] // shards_of).reshape((-1,) + (1,) * (len(dims) - position - 1))

    level = one(*cuts[0])
    for cut in cuts[1:]:
        level = level * one(*cut)
    return level


def length_profile(count, total, most, slope):
    portions = [(1 << 20) // math.isqrt(rank ** slope) + 1 for rank in range(2, count + 1)]
    spare, counts = total - most - (count - 1), [1] * (count - 1)
    while spare > 0:
        candidates = [i for i in range(count - 1) if counts[i] < most]
        pool, budget = sum([portions[i] for i in candidates]), spare
        for i in candidates:
            extra = min(most - counts[i], max(1, budget * portions[i] // pool), spare)
            counts[i] = counts[i] + extra
            spare = spare - extra
    return np.array([most] + counts)


def uneven_parts(own_key, amount, total, most, slope):
    if amount == 2:
        one = jax.random.randint(own_key, (), max(1, total - most), min(most, total - 1) + 1)
        return jnp.stack([one, total - one])
    sizes = jnp.asarray(length_profile(amount, total, most, slope), jnp.int32)
    pairs = (amount - 1) // 2
    donor, sink = sizes[1:1 + 2 * pairs:2], sizes[2:2 + 2 * pairs:2]
    room = jnp.minimum(donor - 1, most - sink)
    shifted = jax.random.randint(jax.random.fold_in(own_key, 1), (pairs,), 0, 1 << 20) % (room + 1)
    sizes = sizes.at[1:1 + 2 * pairs:2].set(donor - shifted).at[2:2 + 2 * pairs:2].set(sink + shifted)
    return sizes[jax.random.permutation(jax.random.fold_in(own_key, 2), amount)]


def scatter_about(own_key, extent, scale, most, shards=(), kind=jnp.bfloat16):
    loudness = steps_of(own_key, extent, shards, -0.22, 0.18) if shards else 1.0
    values = jax.random.normal(own_key, extent, jnp.float32) * scale * loudness
    return jnp.minimum(jnp.maximum(values, -most), most).astype(kind)


def setup_inputs(seed: int = 0) -> dict:
    splits = jax.random.split(jax.random.key(seed), 7)
    latent = draw_latent(jax.random.fold_in(splits[6], 71), 0)
    queries = draw_queries(jax.random.fold_in(splits[6], 71), 0)
    out_grad = scatter_about(splits[2], (GROUPS, SEQ, HEADS * D_NOPE), 1.0, 6.0, ((0, 4), (1, 32), (2, 4)))
    segment_ids = jax.vmap(lambda own: jnp.searchsorted(jnp.cumsum(uneven_parts(own, SEQ // TOK_DEV, SEQ, MOST, 2)), jnp.arange(SEQ), side="right"))(jax.random.split(splits[3], GROUPS)).reshape((GROUPS, SEQ)).astype(jnp.int32)
    key_up = scatter_about(splits[4], (D_LAT, HEADS * D_NOPE), D_LAT ** -0.5, 0.25, ((0, 4), (1, 4)))
    value_up = scatter_about(splits[5], (D_LAT, HEADS * D_NOPE), D_LAT ** -0.5, 0.25, ((0, 4), (1, 4)))
    return {"latent": latent, "queries": queries, "out_grad": out_grad, "segment_ids": segment_ids, "key_up": key_up, "value_up": value_up}


def attend(query_block, grad_block, key_window, value_window, rope_window, allowed, score_scale):
    nope_width = value_window.shape[-1]
    query_all = query_block.astype(jnp.float32)
    query_nope = query_all[:, :, :nope_width]
    query_rope = query_all[:, :, nope_width:]
    key_float = key_window.astype(jnp.float32)
    value_float = value_window.astype(jnp.float32)
    rope_float = rope_window.astype(jnp.float32)
    grad_float = grad_block.astype(jnp.float32)
    scores = (jnp.einsum("ihd,jhd->hij", query_nope, key_float) + jnp.einsum("ihd,jd->hij", query_rope, rope_float)) * score_scale
    scores = jnp.where(allowed[None], scores, -1e30)
    row_max = jnp.max(scores, axis=-1, keepdims=True)
    numerator = jnp.exp(scores - row_max)
    weights = numerator / jnp.sum(numerator, axis=-1, keepdims=True)
    weights_low = weights.astype(jnp.bfloat16).astype(jnp.float32)
    attended = jnp.einsum("hij,jhd->ihd", weights_low, value_float)
    out_dot = jnp.sum(grad_float * attended, axis=-1)
    prob_grad = jnp.einsum("ihd,jhd->hij", grad_float, value_float)
    score_grad = (score_scale * weights * (prob_grad - jnp.transpose(out_dot)[:, :, None])).astype(jnp.bfloat16).astype(jnp.float32)
    query_grad = jnp.concatenate([jnp.einsum("hij,jhd->ihd", score_grad, key_float), jnp.einsum("hij,jd->ihd", score_grad, rope_float)], axis=-1)
    key_grad = jnp.einsum("hij,ihd->jhd", score_grad, query_nope).astype(jnp.bfloat16)
    rope_grad = jnp.einsum("hij,ihd->jd", score_grad, query_rope)
    value_grad = jnp.einsum("hij,ihd->jhd", weights_low, grad_float).astype(jnp.bfloat16)
    return query_grad, key_grad, value_grad, rope_grad


def reference(latent, queries, out_grad, segment_ids, key_up, value_up):
    score_scale = (D_NOPE + D_ROPE) ** -0.5
    margin = REACH * TOK_DEV
    window_rows = (REACH + 1) * TOK_DEV
    blocks = SEQ // TOK_DEV
    key_cols = HEADS * D_NOPE
    w_key32 = key_up.astype(jnp.float32)
    w_value32 = value_up.astype(jnp.float32)
    query_out = []
    latent_out = []
    key_up_grad = jnp.zeros((D_LAT, key_cols), jnp.float32)
    for group in range(GROUPS):
        compressed = latent[group, :, :D_LAT]
        rope_keys = latent[group, :, D_LAT:]
        key_all = jnp.dot(compressed, key_up, preferred_element_type=jnp.float32).astype(jnp.bfloat16).reshape(SEQ, HEADS, D_NOPE)
        value_all = jnp.dot(compressed, value_up, preferred_element_type=jnp.float32).astype(jnp.bfloat16).reshape(SEQ, HEADS, D_NOPE)
        key_pad = jnp.concatenate([jnp.zeros((margin, HEADS, D_NOPE), jnp.bfloat16), key_all], axis=0)
        value_pad = jnp.concatenate([jnp.zeros((margin, HEADS, D_NOPE), jnp.bfloat16), value_all], axis=0)
        rope_pad = jnp.concatenate([jnp.zeros((margin, D_ROPE), jnp.bfloat16), rope_keys], axis=0)
        seg_pad = jnp.concatenate([jnp.full((margin,), -1, jnp.int32), segment_ids[group].astype(jnp.int32)], axis=0)
        query_all = queries[group].reshape(SEQ, HEADS, D_NOPE + D_ROPE)
        grad_all = out_grad[group].reshape(SEQ, HEADS, D_NOPE)

        def block_step(carry, block):
            key_acc, value_acc, rope_acc = carry
            start = (block * TOK_DEV).astype(jnp.int32)
            query_block = lax.dynamic_slice_in_dim(query_all, start, TOK_DEV, 0)
            grad_block = lax.dynamic_slice_in_dim(grad_all, start, TOK_DEV, 0)
            key_window = lax.dynamic_slice_in_dim(key_pad, start, window_rows, 0)
            value_window = lax.dynamic_slice_in_dim(value_pad, start, window_rows, 0)
            rope_window = lax.dynamic_slice_in_dim(rope_pad, start, window_rows, 0)
            query_segments = lax.dynamic_slice_in_dim(seg_pad, start + margin, TOK_DEV, 0)
            key_segments = lax.dynamic_slice_in_dim(seg_pad, start, window_rows, 0)
            query_positions = start + jnp.arange(TOK_DEV, dtype=jnp.int32)
            key_positions = start - margin + jnp.arange(window_rows, dtype=jnp.int32)
            allowed = (key_positions[None, :] <= query_positions[:, None]) & (key_segments[None, :] == query_segments[:, None])
            query_grad, key_grad, value_grad, rope_grad = attend(query_block, grad_block, key_window, value_window, rope_window, allowed, score_scale)
            key_acc = lax.dynamic_update_slice_in_dim(key_acc, lax.dynamic_slice_in_dim(key_acc, start, window_rows, 0) + key_grad.astype(jnp.float32).reshape(window_rows, key_cols), start, 0)
            value_acc = lax.dynamic_update_slice_in_dim(value_acc, lax.dynamic_slice_in_dim(value_acc, start, window_rows, 0) + value_grad.astype(jnp.float32).reshape(window_rows, key_cols), start, 0)
            rope_acc = lax.dynamic_update_slice_in_dim(rope_acc, lax.dynamic_slice_in_dim(rope_acc, start, window_rows, 0) + rope_grad, start, 0)
            return (key_acc, value_acc, rope_acc), query_grad.astype(jnp.bfloat16)

        initial = (jnp.zeros((margin + SEQ, key_cols), jnp.float32), jnp.zeros((margin + SEQ, key_cols), jnp.float32), jnp.zeros((margin + SEQ, D_ROPE), jnp.float32))
        (key_acc, value_acc, rope_acc), query_grads = lax.scan(block_step, initial, jnp.arange(blocks, dtype=jnp.int32))
        key_total = key_acc[margin:]
        value_total = value_acc[margin:]
        rope_total = rope_acc[margin:]
        projected = jnp.dot(key_total, w_key32.T, precision=lax.Precision.HIGHEST) + jnp.dot(value_total, w_value32.T, precision=lax.Precision.HIGHEST)
        latent_out.append(jnp.concatenate([projected, rope_total], axis=1).astype(jnp.bfloat16))
        query_out.append(query_grads.reshape(SEQ, HEADS * (D_NOPE + D_ROPE)))
        key_up_grad = key_up_grad + jnp.dot(compressed.astype(jnp.float32).T, key_total, precision=lax.Precision.HIGHEST)
    return jnp.stack(query_out), jnp.stack(latent_out), key_up_grad
```

```python
import jax
import jax.numpy as jnp
from jax import lax
from jax.experimental import pallas as pl
from jax.experimental.pallas import tpu as pltpu
from jax.sharding import PartitionSpec as P

F32 = jnp.float32
BF16 = jnp.bfloat16
SCALE = (128 + 64) ** -0.5
N_REMOTE = 128
N_LOCAL = 40


def mm(a, b):
    return lax.dot_general(a, b, (((1,), (0,)), ((), ())), preferred_element_type=F32)


def mm_nt(a, b):
    return lax.dot_general(a, b, (((1,), (1,)), ((), ())), preferred_element_type=F32)


def mm_tn(a, b):
    return lax.dot_general(a, b, (((0,), (0,)), ((), ())), preferred_element_type=F32)


def rows(start, size):
    return pl.ds(pl.multiple_of(start, size), size)


def cols(start, size):
    return pl.ds(pl.multiple_of(start, 128), size)


def kernel(
    lat_in, qry_in, grd_in, seg_in, wk_in, wv_in,
    qg_out, lg_out, ku_out,
    wk, wv, qs, gs, lat, seg, bias, ctp, rope0, rope1, kx, vx, dq, u, lacc, racc, dkp, dvp,
    ra, rb, rla, rlb, rra, rrb, sa, sb, tb, za, zp, zb, lb, p1, l2, p2, fl,
    send_sem, recv_sem, local_sem,
):
    s = lax.axis_index("ctx")
    y = lax.axis_index("head")
    x = lax.axis_index("dp")
    z = s // 2
    c = s % 2
    oc = 1 - c
    par = z % 2
    n_z = lax.axis_size("ctx") // 2
    order = [par, 2 + par, 1 - par, 3 - par]

    def at(dz=0, core=None, x_to=None, y_to=None):
        core = c if core is None else core
        zt = (z + dz + n_z) % n_z
        return {
            "ctx": zt * 2 + core,
            "head": y if y_to is None else y_to,
            "dp": x if x_to is None else x_to,
        }

    right, left, far = (x + 1) % 4, (x + 3) % 4, (x + 2) % 4
    pair = at(core=oc)
    sends = []
    locals_ = []
    count = [0, 0]

    def push(src, dst, dev):
        i = count[0]
        count[0] += 1
        copy = pltpu.make_async_remote_copy(
            src_ref=src, dst_ref=dst, send_sem=send_sem.at[i], recv_sem=recv_sem.at[i],
            device_id=dev, device_id_type=pl.DeviceIdType.MESH,
        )
        copy.start()
        sends.append(copy)
        return copy

    def local(src, dst):
        i = count[1]
        count[1] += 1
        copy = pltpu.make_async_copy(src, dst, local_sem.at[i])
        copy.start()
        return copy

    l_lat = [local(lat_in, lat.at[rows((2 + c) * 128, 128)])]
    l_w, l_q = [], []
    for p in order:
        l_w.append((
            local(wk_in.at[:, cols(c * 1024 + p * 256, 256)], wk.at[p, rows(x * 128, 128)]),
            local(wv_in.at[:, cols(c * 1024 + p * 256, 256)], wv.at[p, rows(x * 128, 128)]),
        ))
        l_q.append((
            local(qry_in.at[:, cols(c * 1536 + p * 384, 384)], qs.at[p, rows(c * 128, 128)]),
            local(grd_in.at[:, cols(c * 1024 + p * 256, 256)], gs.at[p, rows(c * 128, 128)]),
        ))
    seg[2 + c] = seg_in[...]

    partners = [pair, at(x_to=right), at(x_to=left)]
    partners += [at(dz=d) for d in (1, -1, 2, -2)]
    partners += [at(dz=4 * d, core=(c if dc == 0 else oc)) for d in (1, 2, 3) for dc in (0, 1)]
    for dy in (1, 2, 3):
        yt = (y + dy) % 4
        partners += [at(y_to=yt), at(dz=-1, y_to=yt), at(dz=1, y_to=yt)]
    barrier = pltpu.get_barrier_semaphore()
    for dev in partners:
        pl.semaphore_signal(barrier, inc=1, device_id=dev, device_id_type=pl.DeviceIdType.MESH)
    pl.semaphore_wait(barrier, len(partners))

    def push_direct(k):
        p = order[k]
        out = []
        for w_in, w in ((wk_in, wk), (wv_in, wv)):
            src = w_in.at[:, cols(c * 1024 + p * 256, 256)]
            dst = w.at[p, rows(x * 128, 128)]
            out.append((push(src, dst, at(x_to=right)), push(src, dst, at(x_to=left))))
        return out

    direct = [push_direct(0)]
    lat_z = push(lat_in, lat.at[rows(c * 128, 128)], at(dz=1))
    seg_z = push(seg_in, seg.at[c], at(dz=1))
    lat_p = push(lat_in, lat.at[rows((2 + c) * 128, 128)], pair)
    seg_p = push(seg_in, seg.at[2 + c], pair)

    def push_tokens(k):
        p = order[k]
        return (
            push(qry_in.at[:, cols(oc * 1536 + p * 384, 384)], qs.at[p, rows(c * 128, 128)], pair),
            push(grd_in.at[:, cols(oc * 1024 + p * 256, 256)], gs.at[p, rows(c * 128, 128)], pair),
        )

    tokens = [push_tokens(0)]

    def forward_x(k):
        p = order[k]
        for pushed in direct[k]:
            for copy in pushed:
                copy.wait_recv()
        mine_k = wk.at[p, rows(left * 128, 128)]
        mine_v = wv.at[p, rows(right * 128, 128)]
        return push(mine_k, mine_k, at(x_to=right)), push(mine_v, mine_v, at(x_to=left))

    def forward_z(k):
        p = order[k]
        out = []
        for xs in (left, right, far):
            piece_k = wk.at[p, rows(xs * 128, 128)]
            piece_v = wv.at[p, rows(xs * 128, 128)]
            out.append(push(piece_k, piece_k, at(dz=1)))
            out.append(push(piece_v, piece_v, at(dz=-1)))
        return out

    lat_z.wait_recv()
    lat_f = push(lat.at[rows(c * 128, 128)], lat.at[rows(c * 128, 128)], pair)
    seg_z.wait_recv()
    seg_f = push(seg.at[c], seg.at[c], pair)

    xf0 = forward_x(0)
    direct.append(push_direct(1))
    for k in (1, 2, 3):
        tokens.append(push_tokens(k))

    seg_p.wait_recv()
    seg_f.wait_recv()
    for kb in range(4):
        key_seg = seg[kb].astype(F32)
        if kb < 2:
            key_seg = jnp.where(z == 0, -1.0, key_seg)
        key_seg = jnp.broadcast_to(key_seg, (128, 128)).T
        for qb in range(2):
            query_seg = jnp.broadcast_to(seg[2 + qb].astype(F32), (128, 128))
            j = kb * 128 + lax.broadcasted_iota(jnp.int32, (128, 128), 0)
            i = (2 + qb) * 128 + lax.broadcasted_iota(jnp.int32, (128, 128), 1)
            allowed = (j <= i) & (key_seg == query_seg)
            bias[kb * 128:(kb + 1) * 128, qb * 128:(qb + 1) * 128] = jnp.where(allowed, 0.0, -1e30)

    l_lat[0].wait()
    lat_p.wait_recv()
    lat_f.wait_recv()
    r = lax.broadcasted_iota(jnp.int32, (512, 512), 0)
    source = 32 * (4 * ((r >> 3) & 3) + ((r >> 5) & 3)) + 16 * ((r >> 2) & 1) + 4 * (r >> 7) + (r & 3)
    to_owner = jnp.where(lax.broadcasted_iota(jnp.int32, (512, 512), 1) == source, 1.0, 0.0).astype(BF16)
    ctp[...] = mm_nt(to_owner, lat[:, :512]).astype(BF16)
    e_row = lax.broadcasted_iota(jnp.int32, (64, 128), 0)
    e_col = lax.broadcasted_iota(jnp.int32, (64, 128), 1)
    rope_keys = lat[:, 512:576]
    rope0[...] = mm(rope_keys, jnp.where(e_col == e_row, 1.0, 0.0).astype(BF16)).astype(BF16)
    rope1[...] = mm(rope_keys, jnp.where(e_col == e_row + 64, 1.0, 0.0).astype(BF16))
    lacc[...] = jnp.zeros_like(lacc)
    racc[...] = jnp.zeros_like(racc)
    low_half = lax.broadcasted_iota(jnp.int32, (512, 128), 1) < 64

    def compute(k, between):
        p = order[k]
        for copy in l_w[k] + l_q[k]:
            copy.wait()
        for copy in tokens[k]:
            copy.wait_recv()
        keys = mm(lat[:, :512], wk[p])
        turned = pltpu.roll(keys[:, 128:], 64, 1)
        kx[0, :, :128] = keys[:, :128].astype(BF16)
        kx[0, :, 128:] = rope0[...]
        kx[1, :, :128] = jnp.where(low_half, 0.0, turned).astype(BF16)
        kx[1, :, 128:] = jnp.where(low_half, turned, rope1[...]).astype(BF16)
        vx[...] = mm(lat[:, :512], wv[p]).astype(BF16)
        dqs = []
        for h in range(2):
            qx = qs[p, :, 128 * h:128 * h + 256]
            gh = gs[p, :, 128 * h:128 * h + 128]
            scores = mm_nt(kx[h], qx) + bias[...]
            top = jnp.max(scores, axis=0, keepdims=True)
            numer = jnp.exp((scores - top) * SCALE)
            weights = numer * (1.0 / jnp.sum(numer, axis=0, keepdims=True))
            low = weights.astype(BF16)
            prob_grad = mm_nt(vx[:, 128 * h:128 * h + 128], gh)
            out_dot = jnp.sum(low.astype(F32) * prob_grad, axis=0, keepdims=True)
            score_grad = (SCALE * weights * (prob_grad - out_dot)).astype(BF16)
            dvp[:, 128 * h:128 * h + 128] = mm(low, gh).astype(BF16)
            dkx = mm(score_grad, qx)
            if h == 0:
                dkp[:, :128] = dkx[:, :128].astype(BF16)
                racc[...] += dkx[:, 128:]
            else:
                t0 = pltpu.roll(dkx[:, :128], 64, 1)
                t1 = pltpu.roll(dkx[:, 128:], 64, 1)
                dkp[:, 128:] = jnp.where(low_half, t0, t1).astype(BF16)
                racc[...] += t1
            dqs.append(mm_tn(score_grad, kx[h]))
            if h == 0:
                between()
        dq[p, :, :128] = dqs[0][:, :128].astype(BF16)
        dq[p, :, 128:256] = (dqs[0][:, 128:] + dqs[1][:, :128]).astype(BF16)
        dq[p, :, 256:] = dqs[1][:, 128:].astype(BF16)
        u[p] = mm(ctp[...], dkp[...]).astype(BF16)
        lacc[...] += mm_nt(dkp[...], wk[p]) + mm_nt(dvp[...], wv[p])

    def push_queries(k):
        p = order[k]
        where = cols(c * 1536 + p * 384, 384)
        moved = push(dq.at[p, rows(oc * 128, 128)], qg_out.at[:, where], pair)
        return moved, local(dq.at[p, rows(c * 128, 128)], qg_out.at[:, where])

    def step1(k):
        p = order[k]
        return (
            push(u.at[p, rows(far * 128, 128), pl.ds(0, 128)], ra.at[p], at(x_to=right)),
            push(u.at[p, rows(far * 128, 128), pl.ds(128, 128)], rb.at[p], at(x_to=left)),
            push(u.at[p, rows(right * 128, 128), pl.ds(128, 128)], rlb.at[p], at(x_to=right)),
            push(u.at[p, rows(left * 128, 128), pl.ds(0, 128)], rra.at[p], at(x_to=left)),
        )

    def step2(k, first):
        p = order[k]
        first[0].wait_recv()
        sa[p] = (u[p, rows(right * 128, 128), :128].astype(F32) + ra[p].astype(F32)).astype(BF16)
        to_right = push(sa.at[p], rla.at[p], at(x_to=right))
        first[1].wait_recv()
        sb[p] = (u[p, rows(left * 128, 128), 128:].astype(F32) + rb[p].astype(F32)).astype(BF16)
        return to_right, push(sb.at[p], rrb.at[p], at(x_to=left))

    def step3(k, first, second):
        p = order[k]
        for copy in (first[2], first[3], second[0], second[1]):
            copy.wait_recv()
        mine = u[p, rows(x * 128, 128), :].astype(F32)
        a = mine[:, :128] + rla[p].astype(F32) + rra[p].astype(F32)
        b = mine[:, 128:] + rlb[p].astype(F32) + rrb[p].astype(F32)
        tb[p, :, :128] = a.astype(BF16)
        tb[p, :, 128:] = b.astype(BF16)
        out = []
        for i, d in enumerate((-1, 1, 2)):
            part = tb.at[p, rows(((z + d + 4) % 4) * 32, 32)]
            out.append(push(part, za.at[i, p], at(dz=d)))
        return out

    for copy in xf0:
        copy.wait_recv()
    zf0 = forward_z(0)
    xf1 = []
    queries = []
    compute(0, lambda: xf1.extend(forward_x(1)))
    queries.append(push_queries(0))
    a0 = step1(0)
    for copy in xf1:
        copy.wait_recv()
    zf1 = forward_z(1)
    compute(1, lambda: None)
    queries.append(push_queries(1))
    a1 = step1(1)
    b0 = step2(0, a0)
    for copy in zf0:
        copy.wait_recv()
    compute(2, lambda: None)
    queries.append(push_queries(2))
    a2 = step1(2)
    b1 = step2(1, a1)
    c0 = step3(0, a0, b0)
    for copy in zf1:
        copy.wait_recv()
    compute(3, lambda: None)
    a3 = step1(3)
    for block in range(4):
        at_rows = slice(block * 128, block * 128 + 128)
        lb[block, :, :512] = lacc[at_rows, :].astype(BF16)
        lb[block, :, 512:576] = racc[at_rows, :64].astype(BF16)
    h1 = push(lb.at[oc], p1.at[0], pair), push(lb.at[2 + oc], p1.at[1], pair)
    queries.append(push_queries(3))
    b2 = step2(2, a2)
    c1 = step3(1, a1, b1)
    b3 = step2(3, a3)
    h2 = []
    for i in range(2):
        h1[i].wait_recv()
        l2[i] = (lb[2 * i + c].astype(F32) + p1[i].astype(F32)).astype(BF16)
        for dy in range(4):
            yt = (y + dy) % 4
            if i == 1 and dy == 0:
                continue
            h2.append(push(l2.at[i, rows(yt * 32, 32)], p2.at[i * 4 + dy], at(dz=i - 1, y_to=yt)))
    c2 = step3(2, a2, b2)
    c3 = step3(3, a3, b3)
    for copy in h2:
        copy.wait_recv()
    total = l2[1, rows(y * 32, 32), :].astype(F32)
    for i in (0, 1, 2, 3, 5, 6, 7):
        total = total + p2[i].astype(F32)
    fl[...] = total.astype(BF16)
    h3 = [push(fl, lg_out.at[rows(y * 32, 32)], at(y_to=(y + dy) % 4)) for dy in (1, 2, 3)]
    l_fl = local(fl, lg_out.at[rows(y * 32, 32)])

    stacked = []
    for p in range(4):
        stacked.append(tb[p, rows((z % 4) * 32, 32), :].astype(F32))
    for copies in (c0, c1, c2, c3):
        for copy in copies:
            copy.wait_recv()
    for p in range(4):
        for i in range(3):
            stacked[p] = stacked[p] + za[i, p].astype(F32)
    stacked = jnp.concatenate(stacked, axis=0).astype(BF16)
    r = lax.broadcasted_iota(jnp.int32, (128, 128), 0)
    source = ((r >> 2) & 3) * 32 + (r >> 4) * 4 + (r & 3)
    regroup = jnp.where(lax.broadcasted_iota(jnp.int32, (128, 128), 1) == source, 1.0, 0.0).astype(BF16)
    regrouped = mm(regroup, stacked).astype(BF16)
    for i in range(8):
        zp[i] = regrouped[16 * i:16 * i + 16]
    h4 = []
    for da in range(4):
        for dc in range(2):
            if da == 0 and dc == 0:
                continue
            core = c if dc == 0 else oc
            piece = (z // 4 + da) % 4 * 2 + core
            h4.append(push(zp.at[piece], zb.at[da * 2 + dc], at(dz=4 * da, core=core)))
    for copy in h4:
        copy.wait_recv()
    for dc in range(2):
        mine = zp[z // 4 * 2 + c] if dc == 0 else zb[dc]
        total = mine.astype(F32)
        for da in (1, 2, 3):
            total = total + zb[da * 2 + dc].astype(F32)
        base = (c if dc == 0 else oc) * 1024
        for p in range(4):
            ku_out[:, cols(base + p * 256, 256)] = total[4 * p:4 * p + 4, :]
    for copy in h3:
        copy.wait_recv()
    l_fl.wait()
    for moved, kept in queries:
        moved.wait_recv()
        kept.wait()
    for copy in sends:
        copy.wait_send()


def local_part(latent, queries, out_grad, segment_ids, key_up, value_up):
    hbm = pl.BlockSpec(memory_space=pl.ANY)
    vmem = pl.BlockSpec(memory_space=pltpu.VMEM)
    V = pltpu.VMEM
    outs = pl.pallas_call(
        kernel,
        out_shape=(
            jax.ShapeDtypeStruct((128, 3072), BF16),
            jax.ShapeDtypeStruct((128, 576), BF16),
            jax.ShapeDtypeStruct((4, 2048), F32),
        ),
        in_specs=[hbm, hbm, hbm, vmem, hbm, hbm],
        out_specs=[hbm, hbm, vmem],
        scratch_shapes=[
            V((4, 512, 256), BF16), V((4, 512, 256), BF16),
            V((4, 256, 384), BF16), V((4, 256, 256), BF16),
            V((512, 576), BF16), V((4, 1, 128), jnp.int32),
            V((512, 256), F32), V((512, 512), BF16),
            V((512, 128), BF16), V((512, 128), F32),
            V((2, 512, 256), BF16), V((512, 256), BF16),
            V((4, 256, 384), BF16), V((4, 512, 256), BF16),
            V((512, 512), F32), V((512, 128), F32),
            V((512, 256), BF16), V((512, 256), BF16),
            V((4, 128, 128), BF16), V((4, 128, 128), BF16),
            V((4, 128, 128), BF16), V((4, 128, 128), BF16),
            V((4, 128, 128), BF16), V((4, 128, 128), BF16),
            V((4, 128, 128), BF16), V((4, 128, 128), BF16),
            V((4, 128, 256), BF16), V((3, 4, 32, 256), BF16),
            V((8, 16, 256), BF16), V((8, 16, 256), BF16),
            V((4, 128, 576), BF16), V((2, 128, 576), BF16),
            V((2, 128, 576), BF16), V((8, 32, 576), BF16),
            V((32, 576), BF16),
            pltpu.SemaphoreType.DMA((N_REMOTE,)),
            pltpu.SemaphoreType.DMA((N_REMOTE,)),
            pltpu.SemaphoreType.DMA((N_LOCAL,)),
        ],
        compiler_params=pltpu.CompilerParams(
            collective_id=0, has_side_effects=True, vmem_limit_bytes=50 * 1024 * 1024
        ),
    )(latent[0], queries[0], out_grad[0], segment_ids, key_up, value_up)
    return outs[0][None], outs[1][None], outs[2]


def solution(mesh):
    return jax.shard_map(
        local_part,
        mesh=mesh,
        in_specs=(
            P("dp", "ctx", None),
            P("dp", "ctx", "head"),
            P("dp", "ctx", "head"),
            P("dp", "ctx"),
            P("dp", "head"),
            P("dp", "head"),
        ),
        out_specs=(P("dp", "ctx", "head"), P("dp", "ctx", None), P(("ctx", "dp"), "head")),
        check_vma=False,
    )
```

```python
import jax
import jax.numpy as jnp
from jax import lax
from jax.experimental import pallas as pl
from jax.experimental.pallas import tpu as pltpu
from jax.sharding import PartitionSpec as P

F32 = jnp.float32
BF16 = jnp.bfloat16
SCALE = (128 + 64) ** -0.5
N_REMOTE = 160
N_LOCAL = 40


def mm(a, b):
    return lax.dot_general(a, b, (((1,), (0,)), ((), ())), preferred_element_type=F32)


def mm_nt(a, b):
    return lax.dot_general(a, b, (((1,), (1,)), ((), ())), preferred_element_type=F32)


def mm_tn(a, b):
    return lax.dot_general(a, b, (((0,), (0,)), ((), ())), preferred_element_type=F32)


def rows(start, size):
    return pl.ds(pl.multiple_of(start, size), size)


def cols(start, size):
    return pl.ds(pl.multiple_of(start, 128), size)


def kernel(
    lat_in, qry_in, grd_in, seg_in, wk_in, wv_in,
    qg_out, lg_out, ku_out,
    wk, wv, qs, gs, latt, lat, seg, bias, ctp, to_owner, rope0, rope1, kx, vx, dq, u, lacc, racc, dkp, dvp,
    ux, tz, zr, ksum, kpeer, lb, p1, l2, p2, fl,
    send_sem, recv_sem, local_sem,
):
    s = lax.axis_index("ctx")
    y = lax.axis_index("head")
    x = lax.axis_index("dp")
    z = s // 2
    c = s % 2
    oc = 1 - c
    par = z % 2
    n_z = lax.axis_size("ctx") // 2
    order = [par, 2 + par, 1 - par, 3 - par]

    def at(dz=0, core=None, x_to=None, y_to=None):
        core = c if core is None else core
        zt = (z + dz + n_z) % n_z
        return {
            "ctx": zt * 2 + core,
            "head": y if y_to is None else y_to,
            "dp": x if x_to is None else x_to,
        }

    right, left, far = (x + 1) % 4, (x + 3) % 4, (x + 2) % 4
    pair = at(core=oc)
    sends = []
    locals_ = []
    count = [0, 0]

    def push(src, dst, dev):
        i = count[0]
        count[0] += 1
        copy = pltpu.make_async_remote_copy(
            src_ref=src, dst_ref=dst, send_sem=send_sem.at[i], recv_sem=recv_sem.at[i],
            device_id=dev, device_id_type=pl.DeviceIdType.MESH,
        )
        copy.start()
        sends.append(copy)
        return copy

    def local(src, dst):
        i = count[1]
        count[1] += 1
        copy = pltpu.make_async_copy(src, dst, local_sem.at[i])
        copy.start()
        return copy

    partners = [pair, at(x_to=right), at(x_to=left), at(x_to=far)]
    partners += [at(dz=d) for d in range(1, 16)]
    for dy in (1, 2, 3):
        yt = (y + dy) % 4
        partners += [at(y_to=yt), at(dz=-1, y_to=yt), at(dz=1, y_to=yt)]
    barrier = pltpu.get_barrier_semaphore()
    for dev in partners:
        pl.semaphore_signal(barrier, inc=1, device_id=dev, device_id_type=pl.DeviceIdType.MESH)

    l_lat = local(lat_in, latt.at[2 + c])
    l_seg = local(seg_in, seg.at[2 + c])
    l_w, l_q = [], []
    for p in order:
        l_w.append((
            local(wk_in.at[:, cols(c * 1024 + p * 256, 256)], wk.at[p, rows(x * 128, 128)]),
            local(wv_in.at[:, cols(c * 1024 + p * 256, 256)], wv.at[p, rows(x * 128, 128)]),
        ))
        l_q.append((
            local(qry_in.at[:, cols(c * 1536 + p * 384, 384)], qs.at[p, rows(c * 128, 128)]),
            local(grd_in.at[:, cols(c * 1024 + p * 256, 256)], gs.at[p, rows(c * 128, 128)]),
        ))

    r = lax.broadcasted_iota(jnp.int32, (512, 512), 0)
    source = 32 * ((r >> 3) & 15) + 16 * ((r >> 2) & 1) + 4 * (r >> 7) + (r & 3)
    to_owner[...] = jnp.where(lax.broadcasted_iota(jnp.int32, (512, 512), 1) == source, 1.0, 0.0).astype(BF16)
    lacc[...] = jnp.zeros_like(lacc)
    racc[...] = jnp.zeros_like(racc)
    pl.semaphore_wait(barrier, len(partners))

    def push_direct(k):
        p = order[k]
        out = []
        for w_in, w in ((wk_in, wk), (wv_in, wv)):
            src = w_in.at[:, cols(c * 1024 + p * 256, 256)]
            out.append([
                push(src, w.at[p, rows(x * 128, 128)], at(x_to=x_to)) for x_to in (far, right, left)
            ])
        return out

    lat_z = push(lat_in, latt.at[c], at(dz=1))
    seg_z = push(seg_in, seg.at[c], at(dz=1))
    direct = [push_direct(0)]
    lat_p = push(lat_in, latt.at[2 + c], pair)
    seg_p = push(seg_in, seg.at[2 + c], pair)

    def push_tokens(k):
        p = order[k]
        return (
            push(qry_in.at[:, cols(oc * 1536 + p * 384, 384)], qs.at[p, rows(c * 128, 128)], pair),
            push(grd_in.at[:, cols(oc * 1024 + p * 256, 256)], gs.at[p, rows(c * 128, 128)], pair),
        )

    tokens = [push_tokens(0)]

    def forward_z(k, part):
        p = order[k]
        w = (wk, wv)[part]
        for copy in direct[k][part]:
            copy.wait_recv()
        out = []
        for start, size, dz in (
            (right * 128, 128, 1), (left * 128, 128, -1), (far * 128, 64, 1), (far * 128 + 64, 64, -1),
        ):
            piece = w.at[p, rows(start, size)]
            out.append(push(piece, piece, at(dz=dz)))
        return out

    lat_z.wait_recv()
    lat_f = push(latt.at[c], latt.at[c], pair)
    seg_z.wait_recv()
    seg_f = push(seg.at[c], seg.at[c], pair)
    direct.append(push_direct(1))
    for k in (1, 2, 3):
        tokens.append(push_tokens(k))

    zf = {(0, 0): forward_z(0, 0)}

    l_seg.wait()
    seg_p.wait_recv()
    seg_f.wait_recv()
    for kb in range(4):
        key_seg = seg[kb].astype(F32)
        if kb < 2:
            key_seg = jnp.where(z == 0, -1.0, key_seg)
        key_seg = jnp.broadcast_to(key_seg, (128, 128)).T
        for qb in range(2):
            query_seg = jnp.broadcast_to(seg[2 + qb].astype(F32), (128, 128))
            j = kb * 128 + lax.broadcasted_iota(jnp.int32, (128, 128), 0)
            i = (2 + qb) * 128 + lax.broadcasted_iota(jnp.int32, (128, 128), 1)
            allowed = (j <= i) & (key_seg == query_seg)
            bias[kb * 128:(kb + 1) * 128, qb * 128:(qb + 1) * 128] = jnp.where(allowed, 0.0, -1e30)

    l_lat.wait()
    lat_p.wait_recv()
    lat_f.wait_recv()
    for block in range(4):
        at_rows = slice(block * 128, block * 128 + 128)
        ctp[:, at_rows] = mm(to_owner[...], latt[block, :512, :]).astype(BF16)
        lat[at_rows, :] = latt[block].T
    e_row = lax.broadcasted_iota(jnp.int32, (64, 128), 0)
    e_col = lax.broadcasted_iota(jnp.int32, (64, 128), 1)
    rope_keys = lat[:, 512:576]
    rope0[...] = mm(rope_keys, jnp.where(e_col == e_row, 1.0, 0.0).astype(BF16)).astype(BF16)
    rope1[...] = mm(rope_keys, jnp.where(e_col == e_row + 64, 1.0, 0.0).astype(BF16))
    low_half = lax.broadcasted_iota(jnp.int32, (512, 128), 1) < 64

    def compute(k, mid, after, finish=lambda: None):
        p = order[k]
        for copy in l_w[k] + l_q[k]:
            copy.wait()
        for copy in tokens[k]:
            copy.wait_recv()
        keys = mm(lat[:, :512], wk[p])
        turned = pltpu.roll(keys[:, 128:], 64, 1)
        kx[0, :, :128] = keys[:, :128].astype(BF16)
        kx[0, :, 128:] = rope0[...]
        kx[1, :, :128] = jnp.where(low_half, 0.0, turned).astype(BF16)
        kx[1, :, 128:] = jnp.where(low_half, turned, rope1[...]).astype(BF16)
        vx[...] = mm(lat[:, :512], wv[p]).astype(BF16)
        grads = []
        for h in range(2):
            qx = qs[p, :, 128 * h:128 * h + 256]
            gh = gs[p, :, 128 * h:128 * h + 128]
            scores = mm_nt(kx[h], qx) + bias[...]
            top = jnp.max(scores, axis=0, keepdims=True)
            numer = jnp.exp((scores - top) * SCALE)
            weights = numer * (1.0 / jnp.sum(numer, axis=0, keepdims=True))
            low = weights.astype(BF16)
            prob_grad = mm_nt(vx[:, 128 * h:128 * h + 128], gh)
            out_dot = jnp.sum(low.astype(F32) * prob_grad, axis=0, keepdims=True)
            score_grad = (SCALE * weights * (prob_grad - out_dot)).astype(BF16)
            dkx = mm(score_grad, qx)
            if h == 0:
                dkp[:, :128] = dkx[:, :128].astype(BF16)
                racc[...] += dkx[:, 128:]
                mid()
            else:
                t0 = pltpu.roll(dkx[:, :128], 64, 1)
                t1 = pltpu.roll(dkx[:, 128:], 64, 1)
                dkp[:, 128:] = jnp.where(low_half, t0, t1).astype(BF16)
                racc[...] += t1
            grads.append((low, gh, score_grad))
        u[p] = mm(ctp[...], dkp[...]).astype(BF16)
        after()
        dqs = []
        for h, (low, gh, score_grad) in enumerate(grads):
            dvp[:, 128 * h:128 * h + 128] = mm(low, gh).astype(BF16)
            dqs.append(mm_tn(score_grad, kx[h]))
        lacc[...] += mm_nt(dkp[...], wk[p]) + mm_nt(dvp[...], wv[p])
        finish()
        dq[p, :, :128] = dqs[0][:, :128].astype(BF16)
        dq[p, :, 128:256] = (dqs[0][:, 128:] + dqs[1][:, :128]).astype(BF16)
        dq[p, :, 256:] = dqs[1][:, 128:].astype(BF16)

    def push_queries(k):
        p = order[k]
        where = cols(c * 1536 + p * 384, 384)
        moved = push(dq.at[p, rows(oc * 128, 128)], qg_out.at[:, where], pair)
        return moved, local(dq.at[p, rows(c * 128, 128)], qg_out.at[:, where])

    def push_x(k):
        p = order[k]
        return [
            push(u.at[p, rows(x_to * 128, 128)], ux.at[i, p], at(x_to=x_to))
            for i, x_to in enumerate((far, right, left))
        ]

    def sum_x(i, arriving):
        p = order[turns[i]]
        for copy in arriving:
            copy.wait_recv()
        total = u[p, rows(x * 128, 128), :].astype(F32)
        for j in range(3):
            total = total + ux[j, p].astype(F32)
        total = total.reshape(16, 8, 256)
        tz[:, i] = jnp.concatenate([total[:, :, :128], total[:, :, 128:]], axis=1).astype(BF16)

    def push_z(first, size):
        out = []
        for d in (8, 7, 9, 6, 10, 5, 11, 4, 12, 3, 13, 2, 14, 1, 15):
            src = tz.at[(z + d) % 16, pl.ds(first, size)]
            out.append(push(src, zr.at[d, pl.ds(first, size)], at(dz=d)))
        return out

    turns = (0, 2, 1, 3)
    queries = []
    over_x = []
    over_z = []
    zf[0, 1] = forward_z(0, 1)

    def pushed_x(k):
        return lambda: over_x.append(push_x(k))

    compute(0, lambda: None, pushed_x(0))
    zf[1, 0] = forward_z(1, 0)
    queries.append(push_queries(0))
    for part in range(2):
        for copy in zf[0, part]:
            copy.wait_recv()
    compute(2, lambda: zf.update({(1, 1): forward_z(1, 1)}), pushed_x(2))
    queries.append(push_queries(2))

    def next_z(i):
        sum_x(i, over_x[i])
        over_z.extend(push_z(i, 1))

    compute(1, lambda: next_z(0), pushed_x(1))
    queries.append(push_queries(1))
    next_z(1)
    for part in range(2):
        for copy in zf[1, part]:
            copy.wait_recv()
    h1 = []

    def start_latent():
        for block in range(4):
            at_rows = slice(block * 128, block * 128 + 128)
            lb[block, :, :512] = lacc[at_rows, :].astype(BF16)
            lb[block, :, 512:576] = racc[at_rows, :64].astype(BF16)
        h1.append(push(lb.at[oc], p1.at[0], pair))
        h1.append(push(lb.at[2 + oc], p1.at[1], pair))

    compute(3, lambda: next_z(2), pushed_x(3), start_latent)
    queries.append(push_queries(3))
    h2 = []
    for i in range(2):
        h1[i].wait_recv()
        l2[i] = (lb[2 * i + c].astype(F32) + p1[i].astype(F32)).astype(BF16)
        for dy in range(4):
            yt = (y + dy) % 4
            if i == 1 and dy == 0:
                continue
            h2.append(push(l2.at[i, rows(yt * 32, 32)], p2.at[i * 4 + dy], at(dz=i - 1, y_to=yt)))
    next_z(3)
    for copy in h2:
        copy.wait_recv()
    total = l2[1, rows(y * 32, 32), :].astype(F32)
    for i in (0, 1, 2, 3, 5, 6, 7):
        total = total + p2[i].astype(F32)
    fl[...] = total.astype(BF16)
    h3 = [push(fl, lg_out.at[rows(y * 32, 32)], at(y_to=(y + dy) % 4)) for dy in (1, 2, 3)]
    l_fl = local(fl, lg_out.at[rows(y * 32, 32)])

    for copy in over_z:
        copy.wait_recv()
    for k in range(4):
        i = turns.index(k)
        other = turns.index((k + 2) % 4)
        total = tz[z, i].astype(F32)
        for d in range(1, 16):
            total = total + zr[d, i if d % 2 == 0 else other].astype(F32)
        ksum[:, cols(order[k] * 256, 128)] = total[:8]
        ksum[:, cols(order[k] * 256 + 128, 128)] = total[8:]
    swap = push(ksum, kpeer, pair)
    ku_out[:, cols(c * 1024, 1024)] = jnp.where(c == 0, ksum[:4, :], ksum[4:, :])
    swap.wait_recv()
    ku_out[:, cols(oc * 1024, 1024)] = jnp.where(c == 0, kpeer[:4, :], kpeer[4:, :])
    for copy in h3:
        copy.wait_recv()
    l_fl.wait()
    for moved, kept in queries:
        moved.wait_recv()
        kept.wait()
    for copy in sends:
        copy.wait_send()


def local_part(latent, queries, out_grad, segment_ids, key_up, value_up):
    hbm = pl.BlockSpec(memory_space=pl.ANY)
    vmem = pl.BlockSpec(memory_space=pltpu.VMEM)
    V = pltpu.VMEM
    outs = pl.pallas_call(
        kernel,
        out_shape=(
            jax.ShapeDtypeStruct((128, 3072), BF16),
            jax.ShapeDtypeStruct((128, 576), BF16),
            jax.ShapeDtypeStruct((4, 2048), F32),
        ),
        in_specs=[hbm] * 6,
        out_specs=[hbm, hbm, vmem],
        scratch_shapes=[
            V((4, 512, 256), BF16), V((4, 512, 256), BF16),
            V((4, 256, 384), BF16), V((4, 256, 256), BF16),
            V((4, 576, 128), BF16), V((512, 576), BF16), V((4, 1, 128), jnp.int32),
            V((512, 256), F32), V((512, 512), BF16), V((512, 512), BF16),
            V((512, 128), BF16), V((512, 128), F32),
            V((2, 512, 256), BF16), V((512, 256), BF16),
            V((4, 256, 384), BF16), V((4, 512, 256), BF16),
            V((512, 512), F32), V((512, 128), F32),
            V((512, 256), BF16), V((512, 256), BF16),
            V((3, 4, 128, 256), BF16),
            V((16, 4, 16, 128), BF16), V((16, 4, 16, 128), BF16),
            V((8, 1024), F32), V((8, 1024), F32),
            V((4, 128, 576), BF16), V((2, 128, 576), BF16),
            V((2, 128, 576), BF16), V((8, 32, 576), BF16),
            V((32, 576), BF16),
            pltpu.SemaphoreType.DMA((N_REMOTE,)),
            pltpu.SemaphoreType.DMA((N_REMOTE,)),
            pltpu.SemaphoreType.DMA((N_LOCAL,)),
        ],
        compiler_params=pltpu.CompilerParams(
            collective_id=0, has_side_effects=True, vmem_limit_bytes=60 * 1024 * 1024
        ),
    )(latent[0].T, queries[0], out_grad[0], segment_ids, key_up, value_up)
    return outs[0][None], outs[1][None], outs[2]


def solution(mesh):
    return jax.shard_map(
        local_part,
        mesh=mesh,
        in_specs=(
            P("dp", "ctx", None),
            P("dp", "ctx", "head"),
            P("dp", "ctx", "head"),
            P("dp", "ctx"),
            P("dp", "head"),
            P("dp", "head"),
        ),
        out_specs=(P("dp", "ctx", "head"), P("dp", "ctx", None), P(("ctx", "dp"), "head")),
        check_vma=False,
    )
```

```python
import jax
import jax.numpy as jnp
from jax import lax
from jax.experimental import pallas as pl
from jax.experimental.pallas import tpu as pltpu
from jax.sharding import PartitionSpec as P

F32 = jnp.float32
BF16 = jnp.bfloat16
SCALE = (128 + 64) ** -0.5
N_REMOTE = 160
N_LOCAL = 40


def mm(a, b):
    return lax.dot_general(a, b, (((1,), (0,)), ((), ())), preferred_element_type=F32)


def mm_nt(a, b):
    return lax.dot_general(a, b, (((1,), (1,)), ((), ())), preferred_element_type=F32)


def mm_tn(a, b):
    return lax.dot_general(a, b, (((0,), (0,)), ((), ())), preferred_element_type=F32)


def rows(start, size):
    return pl.ds(pl.multiple_of(start, size), size)


def cols(start, size):
    return pl.ds(pl.multiple_of(start, 128), size)


def kernel(
    lat_in, qry_in, grd_in, seg_in, wk_in, wv_in,
    qg_out, lg_out, ku_out,
    wk, wv, qs, gs, latt, lat, seg, bias, ctp, to_owner, rope0, rope1, kx, vx, dq, u, lacc, racc, dkp, dvp,
    ux, tz, zr, ksum, kpeer, lb, p1, l2, p2, fl,
    send_sem, recv_sem, local_sem,
):
    s = lax.axis_index("ctx")
    y = lax.axis_index("head")
    x = lax.axis_index("dp")
    z = s // 2
    c = s % 2
    oc = 1 - c
    par = z % 2
    n_z = lax.axis_size("ctx") // 2
    order = [par, 2 + par, 1 - par, 3 - par]

    def at(dz=0, core=None, x_to=None, y_to=None):
        core = c if core is None else core
        zt = (z + dz + n_z) % n_z
        return {
            "ctx": zt * 2 + core,
            "head": y if y_to is None else y_to,
            "dp": x if x_to is None else x_to,
        }

    right, left, far = (x + 1) % 4, (x + 3) % 4, (x + 2) % 4
    pair = at(core=oc)
    sends = []
    locals_ = []
    count = [0, 0]

    def push(src, dst, dev):
        i = count[0]
        count[0] += 1
        copy = pltpu.make_async_remote_copy(
            src_ref=src, dst_ref=dst, send_sem=send_sem.at[i], recv_sem=recv_sem.at[i],
            device_id=dev, device_id_type=pl.DeviceIdType.MESH,
        )
        copy.start()
        sends.append(copy)
        return copy

    def local(src, dst):
        i = count[1]
        count[1] += 1
        copy = pltpu.make_async_copy(src, dst, local_sem.at[i])
        copy.start()
        return copy

    partners = [pair, at(x_to=right), at(x_to=left), at(x_to=far)]
    partners += [at(dz=d) for d in range(1, 16)]
    for dy in (1, 2, 3):
        yt = (y + dy) % 4
        partners += [at(y_to=yt), at(dz=-1, y_to=yt), at(dz=1, y_to=yt)]
    barrier = pltpu.get_barrier_semaphore()
    for dev in partners:
        pl.semaphore_signal(barrier, inc=1, device_id=dev, device_id_type=pl.DeviceIdType.MESH)

    l_lat = local(lat_in, latt.at[2 + c])
    l_seg = local(seg_in, seg.at[2 + c])
    l_w, l_q = [], []
    for p in order:
        l_w.append((
            local(wk_in.at[:, cols(c * 1024 + p * 256, 256)], wk.at[p, rows(x * 128, 128)]),
            local(wv_in.at[:, cols(c * 1024 + p * 256, 256)], wv.at[p, rows(x * 128, 128)]),
        ))
        l_q.append((
            local(qry_in.at[:, cols(c * 1536 + p * 384, 384)], qs.at[p, rows(c * 128, 128)]),
            local(grd_in.at[:, cols(c * 1024 + p * 256, 256)], gs.at[p, rows(c * 128, 128)]),
        ))

    r = lax.broadcasted_iota(jnp.int32, (512, 512), 0)
    source = 32 * ((r >> 3) & 15) + 16 * ((r >> 2) & 1) + 4 * (r >> 7) + (r & 3)
    to_owner[...] = jnp.where(lax.broadcasted_iota(jnp.int32, (512, 512), 1) == source, 1.0, 0.0).astype(BF16)
    lacc[...] = jnp.zeros_like(lacc)
    racc[...] = jnp.zeros_like(racc)
    pl.semaphore_wait(barrier, len(partners))

    def push_direct(k):
        p = order[k]
        out = []
        for w_in, w in ((wk_in, wk), (wv_in, wv)):
            src = w_in.at[:, cols(c * 1024 + p * 256, 256)]
            out.append([
                push(src, w.at[p, rows(x * 128, 128)], at(x_to=x_to)) for x_to in (far, right, left)
            ])
        return out

    lat_z = push(lat_in, latt.at[c], at(dz=1))
    seg_z = push(seg_in, seg.at[c], at(dz=1))
    direct = [push_direct(0)]
    lat_p = push(lat_in, latt.at[2 + c], pair)
    seg_p = push(seg_in, seg.at[2 + c], pair)

    def push_tokens(k):
        p = order[k]
        return (
            push(qry_in.at[:, cols(oc * 1536 + p * 384, 384)], qs.at[p, rows(c * 128, 128)], pair),
            push(grd_in.at[:, cols(oc * 1024 + p * 256, 256)], gs.at[p, rows(c * 128, 128)], pair),
        )

    tokens = [push_tokens(0)]

    def forward_z(k, part):
        p = order[k]
        w = (wk, wv)[part]
        for copy in direct[k][part]:
            copy.wait_recv()
        out = []
        for start, size, dz in (
            (right * 128, 128, 1), (left * 128, 128, -1), (far * 128, 64, 1), (far * 128 + 64, 64, -1),
        ):
            piece = w.at[p, rows(start, size)]
            out.append(push(piece, piece, at(dz=dz)))
        return out

    lat_z.wait_recv()
    lat_f = push(latt.at[c], latt.at[c], pair)
    seg_z.wait_recv()
    seg_f = push(seg.at[c], seg.at[c], pair)
    direct.append(push_direct(1))
    for k in (1, 2, 3):
        tokens.append(push_tokens(k))

    zf = {(0, 0): forward_z(0, 0)}

    l_seg.wait()
    seg_p.wait_recv()
    seg_f.wait_recv()
    for kb in range(4):
        key_seg = seg[kb].astype(F32)
        if kb < 2:
            key_seg = jnp.where(z == 0, -1.0, key_seg)
        key_seg = jnp.broadcast_to(key_seg, (128, 128)).T
        for qb in range(2):
            query_seg = jnp.broadcast_to(seg[2 + qb].astype(F32), (128, 128))
            j = kb * 128 + lax.broadcasted_iota(jnp.int32, (128, 128), 0)
            i = (2 + qb) * 128 + lax.broadcasted_iota(jnp.int32, (128, 128), 1)
            allowed = (j <= i) & (key_seg == query_seg)
            bias[kb * 128:(kb + 1) * 128, qb * 128:(qb + 1) * 128] = jnp.where(allowed, 0.0, -1e30)

    l_lat.wait()
    lat_p.wait_recv()
    lat_f.wait_recv()
    for block in range(4):
        at_rows = slice(block * 128, block * 128 + 128)
        ctp[:, at_rows] = mm(to_owner[...], latt[block, :512, :]).astype(BF16)
        lat[at_rows, :] = latt[block].T
    e_row = lax.broadcasted_iota(jnp.int32, (64, 128), 0)
    e_col = lax.broadcasted_iota(jnp.int32, (64, 128), 1)
    rope_keys = lat[:, 512:576]
    rope0[...] = mm(rope_keys, jnp.where(e_col == e_row, 1.0, 0.0).astype(BF16)).astype(BF16)
    rope1[...] = mm(rope_keys, jnp.where(e_col == e_row + 64, 1.0, 0.0).astype(BF16))
    low_half = lax.broadcasted_iota(jnp.int32, (512, 128), 1) < 64

    def compute(k, mid, after, finish=lambda: None):
        p = order[k]
        for copy in l_w[k] + l_q[k]:
            copy.wait()
        for copy in tokens[k]:
            copy.wait_recv()
        keys = mm(lat[:, :512], wk[p])
        turned = pltpu.roll(keys[:, 128:], 64, 1)
        kx[0, :, :128] = keys[:, :128].astype(BF16)
        kx[0, :, 128:] = rope0[...]
        kx[1, :, :128] = jnp.where(low_half, 0.0, turned).astype(BF16)
        kx[1, :, 128:] = jnp.where(low_half, turned, rope1[...]).astype(BF16)
        vx[...] = mm(lat[:, :512], wv[p]).astype(BF16)
        grads = []
        for h in range(2):
            qx = qs[p, :, 128 * h:128 * h + 256]
            gh = gs[p, :, 128 * h:128 * h + 128]
            scores = mm_nt(kx[h], qx) + bias[...]
            top = jnp.max(scores, axis=0, keepdims=True)
            numer = jnp.exp((scores - top) * SCALE)
            weights = numer * (1.0 / jnp.sum(numer, axis=0, keepdims=True))
            low = weights.astype(BF16)
            prob_grad = mm_nt(vx[:, 128 * h:128 * h + 128], gh)
            out_dot = jnp.sum(low.astype(F32) * prob_grad, axis=0, keepdims=True)
            score_grad = (SCALE * weights * (prob_grad - out_dot)).astype(BF16)
            dkx = mm(score_grad, qx)
            if h == 0:
                dkp[:, :128] = dkx[:, :128].astype(BF16)
                racc[...] += dkx[:, 128:]
                mid()
            else:
                t0 = pltpu.roll(dkx[:, :128], 64, 1)
                t1 = pltpu.roll(dkx[:, 128:], 64, 1)
                dkp[:, 128:] = jnp.where(low_half, t0, t1).astype(BF16)
                racc[...] += t1
            grads.append((low, gh, score_grad))
        u[p] = mm(ctp[...], dkp[...]).astype(BF16)
        after()
        dqs = []
        for h, (low, gh, score_grad) in enumerate(grads):
            dvp[:, 128 * h:128 * h + 128] = mm(low, gh).astype(BF16)
            dqs.append(mm_tn(score_grad, kx[h]))
        lacc[...] += mm_nt(dkp[...], wk[p]) + mm_nt(dvp[...], wv[p])
        finish()
        dq[p, :, :128] = dqs[0][:, :128].astype(BF16)
        dq[p, :, 128:256] = (dqs[0][:, 128:] + dqs[1][:, :128]).astype(BF16)
        dq[p, :, 256:] = dqs[1][:, 128:].astype(BF16)

    def push_queries(k):
        p = order[k]
        where = cols(c * 1536 + p * 384, 384)
        moved = push(dq.at[p, rows(oc * 128, 128)], qg_out.at[:, where], pair)
        return moved, local(dq.at[p, rows(c * 128, 128)], qg_out.at[:, where])

    def push_x(k):
        p = order[k]
        return [
            push(u.at[p, rows(x_to * 128, 128)], ux.at[i, p], at(x_to=x_to))
            for i, x_to in enumerate((far, right, left))
        ]

    def sum_x(i, arriving):
        p = order[turns[i]]
        for copy in arriving:
            copy.wait_recv()
        total = u[p, rows(x * 128, 128), :].astype(F32)
        for j in range(3):
            total = total + ux[j, p].astype(F32)
        total = total.reshape(16, 8, 256)
        tz[:, i] = jnp.concatenate([total[:, :, :128], total[:, :, 128:]], axis=1).astype(BF16)

    def push_z(first, size):
        out = []
        for d in (8, 7, 9, 6, 10, 5, 11, 4, 12, 3, 13, 2, 14, 1, 15):
            src = tz.at[(z + d) % 16, pl.ds(first, size)]
            out.append(push(src, zr.at[d, pl.ds(first, size)], at(dz=d)))
        return out

    turns = (0, 2, 1, 3)
    queries = []
    over_x = []
    over_z = []
    zf[0, 1] = forward_z(0, 1)

    def pushed_x(k):
        return lambda: over_x.append(push_x(k))

    compute(0, lambda: None, pushed_x(0))
    zf[1, 0] = forward_z(1, 0)
    queries.append(push_queries(0))
    for part in range(2):
        for copy in zf[0, part]:
            copy.wait_recv()
    compute(2, lambda: zf.update({(1, 1): forward_z(1, 1)}), pushed_x(2))
    queries.append(push_queries(2))

    def next_z(i):
        sum_x(i, over_x[i])
        over_z.extend(push_z(i, 1))

    compute(1, lambda: next_z(0), pushed_x(1))
    queries.append(push_queries(1))
    next_z(1)
    for part in range(2):
        for copy in zf[1, part]:
            copy.wait_recv()
    h1 = []

    def start_latent():
        for block in range(4):
            at_rows = slice(block * 128, block * 128 + 128)
            lb[block, :, :512] = lacc[at_rows, :].astype(BF16)
            lb[block, :, 512:576] = racc[at_rows, :64].astype(BF16)
        h1.append(push(lb.at[oc], p1.at[0], pair))
        h1.append(push(lb.at[2 + oc], p1.at[1], pair))

    compute(3, lambda: next_z(2), pushed_x(3), start_latent)
    queries.append(push_queries(3))
    h2 = []
    for i in range(2):
        h1[i].wait_recv()
        l2[i] = (lb[2 * i + c].astype(F32) + p1[i].astype(F32)).astype(BF16)
        for dy in range(4):
            yt = (y + dy) % 4
            if i == 1 and dy == 0:
                continue
            h2.append(push(l2.at[i, rows(yt * 32, 32)], p2.at[i * 4 + dy], at(dz=i - 1, y_to=yt)))
    next_z(3)
    for copy in h2:
        copy.wait_recv()
    total = l2[1, rows(y * 32, 32), :].astype(F32)
    for i in (0, 1, 2, 3, 5, 6, 7):
        total = total + p2[i].astype(F32)
    fl[...] = total.astype(BF16)
    h3 = [push(fl, lg_out.at[rows(y * 32, 32)], at(y_to=(y + dy) % 4)) for dy in (1, 2, 3)]
    l_fl = local(fl, lg_out.at[rows(y * 32, 32)])

    for ks, arriving in (((0, 2), over_z[:30]), ((1, 3), over_z[30:])):
        for copy in arriving:
            copy.wait_recv()
        for k in ks:
            i = turns.index(k)
            other = turns.index((k + 2) % 4)
            total = tz[z, i].astype(F32)
            for d in range(1, 16):
                total = total + zr[d, i if d % 2 == 0 else other].astype(F32)
            ksum[:, cols(order[k] * 256, 128)] = total[:8]
            ksum[:, cols(order[k] * 256 + 128, 128)] = total[8:]
    swap = push(ksum, kpeer, pair)
    ku_out[:, cols(c * 1024, 1024)] = jnp.where(c == 0, ksum[:4, :], ksum[4:, :])
    swap.wait_recv()
    ku_out[:, cols(oc * 1024, 1024)] = jnp.where(c == 0, kpeer[:4, :], kpeer[4:, :])
    for copy in h3:
        copy.wait_recv()
    l_fl.wait()
    for moved, kept in queries:
        moved.wait_recv()
        kept.wait()
    for copy in sends:
        copy.wait_send()


def deliver(qg_in, lg_in, ku_in, qg_out, lg_out, ku_out, qg, lg, lgt, ku, sem):
    def copy(src, dst, i):
        started = pltpu.make_async_copy(src, dst, sem.at[i])
        started.start()
        return started

    parts = [pl.ds(16 * i, 16) for i in range(8)]
    latent = copy(lg_in, lg, 0)
    sums = copy(ku_in, ku, 1)
    queries = [copy(qg_in.at[part], qg.at[part], 2 + i) for i, part in enumerate(parts)]
    latent.wait()
    lgt[...] = lg[...].T
    out = [copy(lgt, lg_out, 10)]
    sums.wait()
    out.append(copy(ku, ku_out, 11))
    for i, part in enumerate(parts):
        queries[i].wait()
        out.append(copy(qg.at[part], qg_out.at[part], 12 + i))
    for started in out:
        started.wait()


def local_part(latent, queries, out_grad, segment_ids, key_up, value_up):
    hbm = pl.BlockSpec(memory_space=pl.ANY)
    vmem = pl.BlockSpec(memory_space=pltpu.VMEM)
    V = pltpu.VMEM
    outs = pl.pallas_call(
        kernel,
        out_shape=(
            jax.ShapeDtypeStruct((128, 3072), BF16),
            jax.ShapeDtypeStruct((128, 576), BF16),
            jax.ShapeDtypeStruct((4, 2048), F32),
        ),
        in_specs=[hbm] * 6,
        out_specs=[hbm, hbm, vmem],
        scratch_shapes=[
            V((4, 512, 256), BF16), V((4, 512, 256), BF16),
            V((4, 256, 384), BF16), V((4, 256, 256), BF16),
            V((4, 576, 128), BF16), V((512, 576), BF16), V((4, 1, 128), jnp.int32),
            V((512, 256), F32), V((512, 512), BF16), V((512, 512), BF16),
            V((512, 128), BF16), V((512, 128), F32),
            V((2, 512, 256), BF16), V((512, 256), BF16),
            V((4, 256, 384), BF16), V((4, 512, 256), BF16),
            V((512, 512), F32), V((512, 128), F32),
            V((512, 256), BF16), V((512, 256), BF16),
            V((3, 4, 128, 256), BF16),
            V((16, 4, 16, 128), BF16), V((16, 4, 16, 128), BF16),
            V((8, 1024), F32), V((8, 1024), F32),
            V((4, 128, 576), BF16), V((2, 128, 576), BF16),
            V((2, 128, 576), BF16), V((8, 32, 576), BF16),
            V((32, 576), BF16),
            pltpu.SemaphoreType.DMA((N_REMOTE,)),
            pltpu.SemaphoreType.DMA((N_REMOTE,)),
            pltpu.SemaphoreType.DMA((N_LOCAL,)),
        ],
        compiler_params=pltpu.CompilerParams(
            collective_id=0, has_side_effects=True, vmem_limit_bytes=60 * 1024 * 1024
        ),
    )(latent[0].T, queries[0], out_grad[0], segment_ids, key_up, value_up)
    query_grad, latent_grad, key_up_grad = pl.pallas_call(
        deliver,
        out_shape=(
            jax.ShapeDtypeStruct((128, 3072), BF16),
            jax.ShapeDtypeStruct((576, 128), BF16),
            jax.ShapeDtypeStruct((4, 2048), F32),
        ),
        in_specs=[hbm] * 3,
        out_specs=[hbm] * 3,
        scratch_shapes=[
            V((128, 3072), BF16), V((128, 576), BF16), V((576, 128), BF16), V((4, 2048), F32),
            pltpu.SemaphoreType.DMA((20,)),
        ],
        compiler_params=pltpu.CompilerParams(vmem_limit_bytes=60 * 1024 * 1024),
    )(*outs)
    return query_grad[None], latent_grad.T[None], key_up_grad


def solution(mesh):
    return jax.shard_map(
        local_part,
        mesh=mesh,
        in_specs=(
            P("dp", "ctx", None),
            P("dp", "ctx", "head"),
            P("dp", "ctx", "head"),
            P("dp", "ctx"),
            P("dp", "head"),
            P("dp", "head"),
        ),
        out_specs=(P("dp", "ctx", "head"), P("dp", "ctx", None), P(("ctx", "dp"), "head")),
        check_vma=False,
    )
```

```python
import jax
import jax.numpy as jnp
from jax import lax
from jax.experimental import pallas as pl
from jax.experimental.pallas import tpu as pltpu
from jax.sharding import PartitionSpec as P

F32 = jnp.float32
BF16 = jnp.bfloat16
SCALE = (128 + 64) ** -0.5
N_REMOTE = 160
N_LOCAL = 40


def mm(a, b):
    return lax.dot_general(a, b, (((1,), (0,)), ((), ())), preferred_element_type=F32)


def mm_nt(a, b):
    return lax.dot_general(a, b, (((1,), (1,)), ((), ())), preferred_element_type=F32)


def mm_tn(a, b):
    return lax.dot_general(a, b, (((0,), (0,)), ((), ())), preferred_element_type=F32)


def rows(start, size):
    return pl.ds(pl.multiple_of(start, size), size)


def cols(start, size):
    return pl.ds(pl.multiple_of(start, 128), size)


def kernel(
    lat_in, qry_in, grd_in, seg_in, wk_in, wv_in,
    qg_out, lg_out, ku_out,
    wk, wv, qs, gs, latt, lat, seg, bias, ctp, to_owner, rope0, rope1, kx, vx, dq, u, lacc, racc, dkp, dvp,
    ux, tz, zr, ksum, kpeer, lb, p1, l2, p2, fl,
    send_sem, recv_sem, local_sem, known_sem,
):
    s = lax.axis_index("ctx")
    y = lax.axis_index("head")
    x = lax.axis_index("dp")
    z = s // 2
    c = s % 2
    oc = 1 - c
    par = z % 2
    n_z = lax.axis_size("ctx") // 2
    order = [par, 2 + par, 1 - par, 3 - par]

    def at(dz=0, core=None, x_to=None, y_to=None):
        core = c if core is None else core
        zt = (z + dz + n_z) % n_z
        return {
            "ctx": zt * 2 + core,
            "head": y if y_to is None else y_to,
            "dp": x if x_to is None else x_to,
        }

    right, left, far = (x + 1) % 4, (x + 3) % 4, (x + 2) % 4
    pair = at(core=oc)
    sends = []
    locals_ = []
    count = [0, 0]

    def push(src, dst, dev):
        i = count[0]
        count[0] += 1
        copy = pltpu.make_async_remote_copy(
            src_ref=src, dst_ref=dst, send_sem=send_sem.at[i], recv_sem=recv_sem.at[i],
            device_id=dev, device_id_type=pl.DeviceIdType.MESH,
        )
        copy.start()
        sends.append(copy)
        return copy

    def local(src, dst):
        i = count[1]
        count[1] += 1
        copy = pltpu.make_async_copy(src, dst, local_sem.at[i])
        copy.start()
        return copy

    partners = [pair, at(x_to=right), at(x_to=left), at(x_to=far)]
    partners += [at(dz=d) for d in (1, -1, 2, -2)]
    for dy in (1, 2, 3):
        yt = (y + dy) % 4
        partners += [at(y_to=yt), at(dz=-1, y_to=yt), at(dz=1, y_to=yt)]
    barrier = pltpu.get_barrier_semaphore()
    for dev in partners:
        pl.semaphore_signal(barrier, inc=1, device_id=dev, device_id_type=pl.DeviceIdType.MESH)

    l_lat = local(lat_in, latt.at[2 + c])
    l_seg = local(seg_in, seg.at[2 + c])
    l_w, l_q = [], []
    for p in order:
        l_w.append((
            local(wk_in.at[:, cols(c * 1024 + p * 256, 256)], wk.at[p, rows(x * 128, 128)]),
            local(wv_in.at[:, cols(c * 1024 + p * 256, 256)], wv.at[p, rows(x * 128, 128)]),
        ))
        l_q.append((
            local(qry_in.at[:, cols(c * 1536 + p * 384, 384)], qs.at[p, rows(c * 128, 128)]),
            local(grd_in.at[:, cols(c * 1024 + p * 256, 256)], gs.at[p, rows(c * 128, 128)]),
        ))

    r = lax.broadcasted_iota(jnp.int32, (512, 512), 0)
    source = 32 * ((r >> 3) & 15) + 16 * ((r >> 2) & 1) + 4 * (r >> 7) + (r & 3)
    to_owner[...] = jnp.where(lax.broadcasted_iota(jnp.int32, (512, 512), 1) == source, 1.0, 0.0).astype(BF16)
    lacc[...] = jnp.zeros_like(lacc)
    racc[...] = jnp.zeros_like(racc)
    pl.semaphore_wait(barrier, len(partners))

    def tell(i, reach):
        for d in (reach, -reach):
            pl.semaphore_signal(
                known_sem.at[i], inc=1, device_id=at(dz=d), device_id_type=pl.DeviceIdType.MESH
            )

    tell(0, 2)

    def push_direct(k):
        p = order[k]
        out = []
        for w_in, w in ((wk_in, wk), (wv_in, wv)):
            src = w_in.at[:, cols(c * 1024 + p * 256, 256)]
            out.append([
                push(src, w.at[p, rows(x * 128, 128)], at(x_to=x_to)) for x_to in (far, right, left)
            ])
        return out

    lat_z = push(lat_in, latt.at[c], at(dz=1))
    seg_z = push(seg_in, seg.at[c], at(dz=1))
    direct = [push_direct(0)]
    lat_p = push(lat_in, latt.at[2 + c], pair)
    seg_p = push(seg_in, seg.at[2 + c], pair)

    def push_tokens(k):
        p = order[k]
        return (
            push(qry_in.at[:, cols(oc * 1536 + p * 384, 384)], qs.at[p, rows(c * 128, 128)], pair),
            push(grd_in.at[:, cols(oc * 1024 + p * 256, 256)], gs.at[p, rows(c * 128, 128)], pair),
        )

    tokens = [push_tokens(0)]

    def forward_z(k, part):
        p = order[k]
        w = (wk, wv)[part]
        for copy in direct[k][part]:
            copy.wait_recv()
        out = []
        for start, size, dz in (
            (right * 128, 128, 1), (left * 128, 128, -1), (far * 128, 64, 1), (far * 128 + 64, 64, -1),
        ):
            piece = w.at[p, rows(start, size)]
            out.append(push(piece, piece, at(dz=dz)))
        return out

    lat_z.wait_recv()
    lat_f = push(latt.at[c], latt.at[c], pair)
    seg_z.wait_recv()
    seg_f = push(seg.at[c], seg.at[c], pair)
    direct.append(push_direct(1))
    for k in (1, 2, 3):
        tokens.append(push_tokens(k))

    zf = {(0, 0): forward_z(0, 0)}

    pl.semaphore_wait(known_sem.at[0], 2)
    tell(1, 4)

    l_seg.wait()
    seg_p.wait_recv()
    seg_f.wait_recv()
    for kb in range(4):
        key_seg = seg[kb].astype(F32)
        if kb < 2:
            key_seg = jnp.where(z == 0, -1.0, key_seg)
        key_seg = jnp.broadcast_to(key_seg, (128, 128)).T
        for qb in range(2):
            query_seg = jnp.broadcast_to(seg[2 + qb].astype(F32), (128, 128))
            j = kb * 128 + lax.broadcasted_iota(jnp.int32, (128, 128), 0)
            i = (2 + qb) * 128 + lax.broadcasted_iota(jnp.int32, (128, 128), 1)
            allowed = (j <= i) & (key_seg == query_seg)
            bias[kb * 128:(kb + 1) * 128, qb * 128:(qb + 1) * 128] = jnp.where(allowed, 0.0, -1e30)

    l_lat.wait()
    lat_p.wait_recv()
    lat_f.wait_recv()
    for block in range(4):
        at_rows = slice(block * 128, block * 128 + 128)
        ctp[:, at_rows] = mm(to_owner[...], latt[block, :512, :]).astype(BF16)
        lat[at_rows, :] = latt[block].T
    e_row = lax.broadcasted_iota(jnp.int32, (64, 128), 0)
    e_col = lax.broadcasted_iota(jnp.int32, (64, 128), 1)
    rope_keys = lat[:, 512:576]
    rope0[...] = mm(rope_keys, jnp.where(e_col == e_row, 1.0, 0.0).astype(BF16)).astype(BF16)
    rope1[...] = mm(rope_keys, jnp.where(e_col == e_row + 64, 1.0, 0.0).astype(BF16))
    low_half = lax.broadcasted_iota(jnp.int32, (512, 128), 1) < 64

    def compute(k, mid, after, finish=lambda: None):
        p = order[k]
        for copy in l_w[k] + l_q[k]:
            copy.wait()
        for copy in tokens[k]:
            copy.wait_recv()
        keys = mm(lat[:, :512], wk[p])
        turned = pltpu.roll(keys[:, 128:], 64, 1)
        kx[0, :, :128] = keys[:, :128].astype(BF16)
        kx[0, :, 128:] = rope0[...]
        kx[1, :, :128] = jnp.where(low_half, 0.0, turned).astype(BF16)
        kx[1, :, 128:] = jnp.where(low_half, turned, rope1[...]).astype(BF16)
        vx[...] = mm(lat[:, :512], wv[p]).astype(BF16)
        grads = []
        for h in range(2):
            qx = qs[p, :, 128 * h:128 * h + 256]
            gh = gs[p, :, 128 * h:128 * h + 128]
            scores = mm_nt(kx[h], qx) + bias[...]
            top = jnp.max(scores, axis=0, keepdims=True)
            numer = jnp.exp((scores - top) * SCALE)
            weights = numer * (1.0 / jnp.sum(numer, axis=0, keepdims=True))
            low = weights.astype(BF16)
            prob_grad = mm_nt(vx[:, 128 * h:128 * h + 128], gh)
            out_dot = jnp.sum(low.astype(F32) * prob_grad, axis=0, keepdims=True)
            score_grad = (SCALE * weights * (prob_grad - out_dot)).astype(BF16)
            dkx = mm(score_grad, qx)
            if h == 0:
                dkp[:, :128] = dkx[:, :128].astype(BF16)
                racc[...] += dkx[:, 128:]
                mid()
            else:
                t0 = pltpu.roll(dkx[:, :128], 64, 1)
                t1 = pltpu.roll(dkx[:, 128:], 64, 1)
                dkp[:, 128:] = jnp.where(low_half, t0, t1).astype(BF16)
                racc[...] += t1
            grads.append((low, gh, score_grad))
        u[p] = mm(ctp[...], dkp[...]).astype(BF16)
        after()
        dqs = []
        for h, (low, gh, score_grad) in enumerate(grads):
            dvp[:, 128 * h:128 * h + 128] = mm(low, gh).astype(BF16)
            dqs.append(mm_tn(score_grad, kx[h]))
        lacc[...] += mm_nt(dkp[...], wk[p]) + mm_nt(dvp[...], wv[p])
        finish()
        dq[p, :, :128] = dqs[0][:, :128].astype(BF16)
        dq[p, :, 128:256] = (dqs[0][:, 128:] + dqs[1][:, :128]).astype(BF16)
        dq[p, :, 256:] = dqs[1][:, 128:].astype(BF16)

    def push_queries(k):
        p = order[k]
        where = cols(c * 1536 + p * 384, 384)
        moved = push(dq.at[p, rows(oc * 128, 128)], qg_out.at[:, where], pair)
        return moved, local(dq.at[p, rows(c * 128, 128)], qg_out.at[:, where])

    def push_x(k):
        p = order[k]
        return [
            push(u.at[p, rows(x_to * 128, 128)], ux.at[i, p], at(x_to=x_to))
            for i, x_to in enumerate((far, right, left))
        ]

    def sum_x(i, arriving):
        p = order[turns[i]]
        for copy in arriving:
            copy.wait_recv()
        total = u[p, rows(x * 128, 128), :].astype(F32)
        for j in range(3):
            total = total + ux[j, p].astype(F32)
        total = total.reshape(16, 8, 256)
        tz[:, i] = jnp.concatenate([total[:, :, :128], total[:, :, 128:]], axis=1).astype(BF16)

    def push_z(first, size):
        out = []
        for d in (8, 7, 9, 6, 10, 5, 11, 4, 12, 3, 13, 2, 14, 1, 15):
            src = tz.at[(z + d) % 16, pl.ds(first, size)]
            out.append(push(src, zr.at[d, pl.ds(first, size)], at(dz=d)))
        return out

    turns = (0, 2, 1, 3)
    queries = []
    over_x = []
    over_z = []
    zf[0, 1] = forward_z(0, 1)

    def pushed_x(k):
        return lambda: over_x.append(push_x(k))

    compute(0, lambda: None, pushed_x(0))
    pl.semaphore_wait(known_sem.at[1], 2)
    zf[1, 0] = forward_z(1, 0)
    queries.append(push_queries(0))
    for part in range(2):
        for copy in zf[0, part]:
            copy.wait_recv()
    compute(2, lambda: zf.update({(1, 1): forward_z(1, 1)}), pushed_x(2))
    queries.append(push_queries(2))

    def next_z(i):
        sum_x(i, over_x[i])
        over_z.extend(push_z(i, 1))

    compute(1, lambda: next_z(0), pushed_x(1))
    queries.append(push_queries(1))
    next_z(1)
    for part in range(2):
        for copy in zf[1, part]:
            copy.wait_recv()
    h1 = []

    def start_latent():
        for block in range(4):
            at_rows = slice(block * 128, block * 128 + 128)
            lb[block, :, :512] = lacc[at_rows, :].astype(BF16)
            lb[block, :, 512:576] = racc[at_rows, :64].astype(BF16)
        h1.append(push(lb.at[oc], p1.at[0], pair))
        h1.append(push(lb.at[2 + oc], p1.at[1], pair))

    compute(3, lambda: next_z(2), pushed_x(3), start_latent)
    queries.append(push_queries(3))
    h2 = []
    for i in range(2):
        h1[i].wait_recv()
        l2[i] = (lb[2 * i + c].astype(F32) + p1[i].astype(F32)).astype(BF16)
        for dy in range(4):
            yt = (y + dy) % 4
            if i == 1 and dy == 0:
                continue
            h2.append(push(l2.at[i, rows(yt * 32, 32)], p2.at[i * 4 + dy], at(dz=i - 1, y_to=yt)))
    next_z(3)
    for copy in h2:
        copy.wait_recv()
    total = l2[1, rows(y * 32, 32), :].astype(F32)
    for i in (0, 1, 2, 3, 5, 6, 7):
        total = total + p2[i].astype(F32)
    fl[...] = total.astype(BF16)
    h3 = [push(fl, lg_out.at[rows(y * 32, 32)], at(y_to=(y + dy) % 4)) for dy in (1, 2, 3)]
    l_fl = local(fl, lg_out.at[rows(y * 32, 32)])

    for ks, arriving in (((0, 2), over_z[:30]), ((1, 3), over_z[30:])):
        if ks == (1, 3):
            for moved, kept in queries:
                moved.wait_recv()
                kept.wait()
            for copy in sends:
                copy.wait_send()
        for copy in arriving:
            copy.wait_recv()
        for k in ks:
            i = turns.index(k)
            other = turns.index((k + 2) % 4)
            total = tz[z, i].astype(F32)
            for d in range(1, 16):
                total = total + zr[d, i if d % 2 == 0 else other].astype(F32)
            ksum[:, cols(order[k] * 256, 128)] = total[:8]
            ksum[:, cols(order[k] * 256 + 128, 128)] = total[8:]
    swap = push(ksum, kpeer, pair)
    ku_out[:, cols(c * 1024, 1024)] = jnp.where(c == 0, ksum[:4, :], ksum[4:, :])
    swap.wait_recv()
    ku_out[:, cols(oc * 1024, 1024)] = jnp.where(c == 0, kpeer[:4, :], kpeer[4:, :])
    for copy in h3:
        copy.wait_recv()
    l_fl.wait()
    swap.wait_send()


def deliver(qg_in, lg_in, ku_in, qg_out, lg_out, ku_out, qg, lg, lgt, ku, sem):
    def copy(src, dst, i):
        started = pltpu.make_async_copy(src, dst, sem.at[i])
        started.start()
        return started

    parts = [pl.ds(16 * i, 16) for i in range(8)]
    latent = copy(lg_in, lg, 0)
    sums = copy(ku_in, ku, 1)
    queries = [copy(qg_in.at[part], qg.at[part], 2 + i) for i, part in enumerate(parts)]
    latent.wait()
    lgt[...] = lg[...].T
    out = [copy(lgt, lg_out, 10)]
    sums.wait()
    out.append(copy(ku, ku_out, 11))
    for i, part in enumerate(parts):
        queries[i].wait()
        out.append(copy(qg.at[part], qg_out.at[part], 12 + i))
    for started in out:
        started.wait()


def local_part(latent, queries, out_grad, segment_ids, key_up, value_up):
    hbm = pl.BlockSpec(memory_space=pl.ANY)
    vmem = pl.BlockSpec(memory_space=pltpu.VMEM)
    V = pltpu.VMEM
    outs = pl.pallas_call(
        kernel,
        out_shape=(
            jax.ShapeDtypeStruct((128, 3072), BF16),
            jax.ShapeDtypeStruct((128, 576), BF16),
            jax.ShapeDtypeStruct((4, 2048), F32),
        ),
        in_specs=[hbm] * 6,
        out_specs=[hbm, hbm, vmem],
        scratch_shapes=[
            V((4, 512, 256), BF16), V((4, 512, 256), BF16),
            V((4, 256, 384), BF16), V((4, 256, 256), BF16),
            V((4, 576, 128), BF16), V((512, 576), BF16), V((4, 1, 128), jnp.int32),
            V((512, 256), F32), V((512, 512), BF16), V((512, 512), BF16),
            V((512, 128), BF16), V((512, 128), F32),
            V((2, 512, 256), BF16), V((512, 256), BF16),
            V((4, 256, 384), BF16), V((4, 512, 256), BF16),
            V((512, 512), F32), V((512, 128), F32),
            V((512, 256), BF16), V((512, 256), BF16),
            V((3, 4, 128, 256), BF16),
            V((16, 4, 16, 128), BF16), V((16, 4, 16, 128), BF16),
            V((8, 1024), F32), V((8, 1024), F32),
            V((4, 128, 576), BF16), V((2, 128, 576), BF16),
            V((2, 128, 576), BF16), V((8, 32, 576), BF16),
            V((32, 576), BF16),
            pltpu.SemaphoreType.DMA((N_REMOTE,)),
            pltpu.SemaphoreType.DMA((N_REMOTE,)),
            pltpu.SemaphoreType.DMA((N_LOCAL,)),
            pltpu.SemaphoreType.REGULAR((2,)),
        ],
        compiler_params=pltpu.CompilerParams(
            collective_id=0, has_side_effects=True, vmem_limit_bytes=60 * 1024 * 1024
        ),
    )(latent[0].T, queries[0], out_grad[0], segment_ids, key_up, value_up)
    query_grad, latent_grad, key_up_grad = pl.pallas_call(
        deliver,
        out_shape=(
            jax.ShapeDtypeStruct((128, 3072), BF16),
            jax.ShapeDtypeStruct((576, 128), BF16),
            jax.ShapeDtypeStruct((4, 2048), F32),
        ),
        in_specs=[hbm] * 3,
        out_specs=[hbm] * 3,
        scratch_shapes=[
            V((128, 3072), BF16), V((128, 576), BF16), V((576, 128), BF16), V((4, 2048), F32),
            pltpu.SemaphoreType.DMA((20,)),
        ],
        compiler_params=pltpu.CompilerParams(vmem_limit_bytes=60 * 1024 * 1024),
    )(*outs)
    return query_grad[None], latent_grad.T[None], key_up_grad


def solution(mesh):
    return jax.shard_map(
        local_part,
        mesh=mesh,
        in_specs=(
            P("dp", "ctx", None),
            P("dp", "ctx", "head"),
            P("dp", "ctx", "head"),
            P("dp", "ctx"),
            P("dp", "head"),
            P("dp", "head"),
        ),
        out_specs=(P("dp", "ctx", "head"), P("dp", "ctx", None), P(("ctx", "dp"), "head")),
        check_vma=False,
    )
```
